512 devices in a mesh: tm: 64 (over x, z), col: 8 (over y, core).
Axes of the slice: x: 4, y: 4, z: 16, core: 2. Of those that a mesh axis runs over, the one named last changes fastest.
Arguments:
- rhs: float32 [64, 1024, 256], P('tm', 'col'), may hold values from -6 to 6
- inverse_blocks: float32 [3, 64, 1024, 1024], P(None, 'tm', None, 'col'), may hold values from -2 to 3, as said below
- lower_coupling: float32 [3, 64, 1024, 1024], P(None, 'tm', None, 'col'), may hold values from -0.1875 to 0.1875
- upper_coupling: float32 [3, 64, 1024, 1024], P(None, 'tm', None, 'col'), may hold values from -0.1875 to 0.1875
- tile_pattern: int32 [3, 64, 2, 8, 8], P(None, 'tm', None, None, 'col'), may hold values from 0 to 1, as said below
- tip_coupling: float32 [3, 64, 64, 1024], P(None, 'tm', None, 'col'), may hold values from -0.0234375 to 0.0234375
- tip_rhs: float32 [64, 256], replicated, may hold values from -6 to 6
Outputs:
- reduced: float32 [64, 1024, 256], P('tm', 'col')
- tip_reduced: float32 [64, 256], replicated
The draws below stay inside these ranges and needn't reach their ends.
Inputs may be any that keep to these rules, and one draw needn't show every extreme that they name: Every inverse_blocks[l, j] is symmetric. tile_pattern[l, j, k, r, c] is 1 exactly where |r - c| is at most a half-width w[l, j, k] of 1 to 4; both half-widths 1 and 4 occur.
All inputs are finite; a program needn't handle non-finite values.
Results may differ from the reference program's by a relative error of at most 0.0001.
Values sent between devices are 32-bit elements; how exact they have to be, the bound alone decides.
No kernel may reach another device: no remote copies, remote signals or barrier semaphores. Data moves between devices by JAX's collectives and lax.ppermute only.
A program may use at most 64 MiB of HBM per device.

```python
import math
import jax
import jax.numpy as jnp
from jax import lax

B = 1024
F = 64
NT = 8
REDUCTION_DEPTH = 3
R = 256
NB = 64


def draw_inverse_blocks(key, part):
    noise_draw = jnp.clip(jax.random.normal(key, (REDUCTION_DEPTH, NB, B, B), jnp.float32), -6.0, 6.0)
    symmetric = (noise_draw + jnp.swapaxes(noise_draw, 2, 3)) * (0.1 / math.sqrt(2.0 * B))
    diagonal = jnp.exp(jax.random.uniform(jax.random.fold_in(key, 1), (REDUCTION_DEPTH, NB, B), jnp.float32, math.log(0.25), math.log(0.5)))
    blocks = symmetric + diagonal[:, :, :, None] * jnp.eye(B, dtype=jnp.float32)[None, None]
    return blocks


def draw_tile_pattern(key, part):
    widest = NT // 2
    band_width = jax.random.randint(key, (REDUCTION_DEPTH, NB, 2), 1, widest + 1)
    band_width = band_width.at[0, 0, 0].set(1).at[0, 0, 1].set(widest)
    tile_index = jnp.arange(NT)
    tile_gap = jnp.abs(tile_index[:, None] - tile_index[None, :])
    return (tile_gap[None, None, None] <= band_width[:, :, :, None, None]).astype(jnp.int32)


def levels(rng, dims, cuts, least, largest):
    level, own = 1.0, jax.random.fold_in(rng, 6)
    for position, blocks in cuts:
        steps = jnp.exp(jax.random.uniform(jax.random.fold_in(own, position), (blocks,), jnp.float32, least / len(cuts), largest / len(cuts)))
        level = level * jnp.repeat(steps, dims[position] // blocks).reshape([-1 if axis == position else 1 for axis in range(len(dims))])
    return level


def normal_values(own_key, extent, deviation, bound, shards=(), kind=jnp.bfloat16):
    level = levels(own_key, extent, shards, -0.22, 0.18) if shards else 1.0
    drawn = jax.random.normal(own_key, extent, jnp.float32) * deviation * level
    return jnp.minimum(jnp.maximum(drawn, -bound), bound).astype(kind)


def setup_inputs(seed: int = 0) -> dict:
    key_of = jax.random.split(jax.random.key(seed), 8)
    rhs = normal_values(key_of[0], (NB, B, R), 1.0, 6.0, ((0, 64), (1, 8)), jnp.float32)
    inverse_blocks = draw_inverse_blocks(jax.random.fold_in(key_of[7], 71), 0)
    lower_coupling = normal_values(key_of[2], (REDUCTION_DEPTH, NB, B, B), B ** -0.5, 0.1875, ((1, 64), (3, 8)), jnp.float32)
    upper_coupling = normal_values(key_of[3], (REDUCTION_DEPTH, NB, B, B), B ** -0.5, 0.1875, ((1, 64), (3, 8)), jnp.float32)
    tile_pattern = draw_tile_pattern(jax.random.fold_in(key_of[7], 71), 0)
    tip_coupling = normal_values(key_of[5], (REDUCTION_DEPTH, NB, F, B), (B * NB) ** -0.5, 0.0234375, ((1, 64), (3, 8)), jnp.float32)
    tip_rhs = normal_values(key_of[6], (F, R), 1.0, 6.0, (), jnp.float32)
    return {"rhs": rhs, "inverse_blocks": inverse_blocks, "lower_coupling": lower_coupling, "upper_coupling": upper_coupling, "tile_pattern": tile_pattern, "tip_coupling": tip_coupling, "tip_rhs": tip_rhs}


def expand(pattern):
    tile_size = B // NT
    widened = jnp.repeat(pattern.astype(jnp.float32), tile_size, axis=1)
    return jnp.repeat(widened, tile_size, axis=2)


def reference(rhs, inverse_blocks, lower_coupling, upper_coupling, tile_pattern, tip_coupling, tip_rhs):
    highest = lax.Precision.HIGHEST
    present_rows = rhs
    tip_total = tip_rhs
    for level_number in range(REDUCTION_DEPTH):
        stride = 2 ** level_number
        lower_masked = lower_coupling[level_number] * expand(tile_pattern[level_number, :, 0])
        upper_masked = upper_coupling[level_number] * expand(tile_pattern[level_number, :, 1])
        solved = jnp.einsum("jab,jbr->jar", inverse_blocks[level_number], present_rows, precision=highest)
        down_term = jnp.einsum("jba,jbr->jar", lower_masked, solved, precision=highest)
        up_term = jnp.einsum("jba,jbr->jar", upper_masked, solved, precision=highest)
        present_rows = present_rows - jnp.roll(down_term, -stride, axis=0) - jnp.roll(up_term, stride, axis=0)
        tip_total = tip_total - jnp.einsum("jfb,jbr->fr", tip_coupling[level_number], solved, precision=highest)
    return present_rows, tip_total
```

```python
import functools

import jax
import jax.numpy as jnp
from jax import lax
from jax.experimental import pallas as pl
from jax.experimental.pallas import tpu as pltpu
from jax.sharding import PartitionSpec as P

T = 128
CORES = 2
VMEM = pl.BlockSpec(memory_space=pltpu.VMEM)
SMEM = pl.BlockSpec(memory_space=pltpu.SMEM)


def own_core():
    return lax.rem(lax.axis_index("col"), CORES)


def lanes(half):
    return pl.ds(pl.multiple_of(half * T, T), T)


def halves(value):
    high = value.astype(jnp.bfloat16)
    return high, (value - high.astype(jnp.float32)).astype(jnp.bfloat16)


def mul(a, b, dims):
    return lax.dot_general(a, b, (dims, ((), ())), preferred_element_type=jnp.float32)


def product(left, right, dims=((1,), (0,))):
    rows = left.shape[0]
    left_high, left_low = halves(left)
    right_high, right_low = halves(right)
    both = mul(jnp.concatenate([left_high, left_low], axis=0), right_high, dims)
    return both[:rows] + both[rows:] + mul(left_high, right_low, dims)


def call(body, out_shapes, smem, *args):
    return pl.pallas_call(
        body,
        out_shape=[jax.ShapeDtypeStruct(s, jnp.float32) for s in out_shapes],
        in_specs=[SMEM] * smem + [VMEM] * (len(args) - smem),
        out_specs=[VMEM] * len(out_shapes),
        compiler_params=pltpu.CompilerParams(vmem_limit_bytes=16 * 2**20),
    )(*args)


def column_blocks(ref, k):
    return jnp.concatenate([ref[CORES * k + c].T for c in range(CORES)], axis=1)


def own_columns(own, other, level, rows):
    return jnp.concatenate([own[level, 0, rows, :], other[level, 0, rows, :]], axis=1)


def in_order(out, index, value):
    core = own_core()
    out[(*index, lanes(core))] = value[:, :T]
    out[(*index, lanes(1 - core))] = value[:, T:]


def solve(x, level, own, other):
    parts, _, width = x.shape
    total = jnp.zeros((T, width), jnp.float32)
    for k in range(parts):
        total = total + product(x[k, :T, :], own_columns(own, other, level, pl.ds(k * width, width)))
    return total


def tip_term(level, tip_own, tip_other, solved):
    return product(jnp.concatenate([tip_own[level, 0], tip_other[level, 0]], axis=1), solved, ((1,), (1,)))


def first_solve_kernel(x, own, other, tip_own, tip_other, out, tip, entered):
    parts = out.shape[0]
    width = CORES * T
    total = jnp.zeros((T, width), jnp.float32)
    for k in range(parts):
        total = total + product(column_blocks(x, k), own_columns(own, other, 0, pl.ds(k * width, width)))
    for k in range(parts):
        in_order(out, (k, slice(None)), total)
    tip[...] = tip_term(0, tip_own, tip_other, total)
    chip = lax.div(lax.axis_index("col"), CORES)
    for c in range(CORES):
        entered[:, c * T : (c + 1) * T] = x[CORES * chip + c].T


def solve_kernel(level, x, own, other, tip_own, tip_other, tip_before, out, tip):
    total = solve(x, level, own, other)
    for k in range(out.shape[0]):
        in_order(out, (k, slice(None)), total)
    tip[...] = tip_before[...] + tip_term(level, tip_own, tip_other, total)


def last_solve_kernel(level, x, own, other, tip_own, tip_other, tip_before, out):
    parts = out.shape[0]
    height = out.shape[1] - T
    total = solve(x, level, own, other)
    tip = tip_before[...] + tip_term(level, tip_own, tip_other, total)
    for k in range(parts):
        in_order(out, (k, slice(0, T)), total)
        for c in range(CORES):
            first = (CORES * k + c) * height
            out[k, pl.ds(T, height), c * T : (c + 1) * T] = tip[first : first + height]


def advance_kernel(x, above, below, out, x_out):
    now = x[...] - above[...] - below[...]
    x_out[...] = now
    for k in range(out.shape[0]):
        out[k] = now


def couple_kernel(level, pattern, s, low_own, low_other, up_own, up_other, down, up, *tip_out):
    core = own_core()
    column = lax.axis_index("col")
    beside = column + 1 - 2 * core
    parts = s.shape[0]
    width = CORES * T
    tiles = CORES * parts
    for which, (own, other, out) in enumerate(((low_own, low_other, down), (up_own, up_other, up))):
        base = (level * 2 + which) * tiles
        here = [pattern[base + r] for r in range(tiles)]
        reach = jnp.int32(0)
        for r in range(tiles):
            reach = jnp.maximum(reach, jnp.where(here[r] > 0, jnp.abs(r - column), 0))
        total = jnp.zeros((T, width), jnp.float32)
        for k in range(parts):
            blocks = []
            for r in (CORES * k, CORES * k + 1):
                rows = pl.ds(r * T, T)
                near = jnp.where(jnp.abs(r - beside) <= reach, 1.0, 0.0).astype(jnp.float32)
                blocks.append(
                    jnp.concatenate(
                        [
                            own[level, 0, rows, :] * here[r].astype(jnp.float32),
                            other[level, 0, rows, :] * near,
                        ],
                        axis=1,
                    )
                )
            total = total + product(s[k, :T, :], jnp.concatenate(blocks, axis=0))
        in_order(out, (slice(None),), total)


    if tip_out:
        count, height, _ = tip_out[0].shape
        tip = sum(s[k, pl.ds(T, height), :] for k in range(parts))
        for i in range(count):
            tip_out[0][i] = tip


def leave_kernel(x, above, below, keep, send):
    core = own_core()
    for half, out in ((core, keep), (1 - core, send)):
        out[...] = x[:, lanes(half)] - above[:, lanes(half)] - below[:, lanes(half)]


def place_kernel(keep, received, out):
    core = own_core()
    out[0, :, lanes(core)] = keep[...].T
    out[0, :, lanes(1 - core)] = received[...].T


def tip_kernel(chips, tip_rhs, parts, out):
    height = parts.shape[1]
    count = parts.shape[0] // (CORES * chips)
    for chip in range(chips):
        for core in range(CORES):
            place = CORES * chip + core
            total = sum(parts[CORES * chips * q + place] for q in range(count))
            columns = pl.ds(core * T, T)
            for c in range(CORES):
                rows = pl.ds((CORES * chip + c) * height, height)
                out[rows, columns] = tip_rhs[rows, columns] - total[:, c * T : (c + 1) * T]


def passed(block, axis, target):
    return lax.ppermute(block, axis, [(i, target(i)) for i in range(lax.axis_size(axis))])


def local(rhs, inverse_blocks, lower_coupling, upper_coupling, tile_pattern, tip_coupling, tip_rhs):
    levels = inverse_blocks.shape[0]
    fixed = tip_rhs.shape[0]
    columns, rows = lax.axis_size("col"), lax.axis_size("tm")
    chips = columns // CORES
    width = CORES * T
    core = own_core()
    same_core = [[c + CORES * k for k in range(chips)] for c in range(CORES)]

    def swapped(block):
        return passed(block, "col", lambda i: i ^ 1)

    def exchanged(block):
        return lax.all_to_all(block, "col", 0, 0, axis_index_groups=same_core, tiled=True)

    pattern = tile_pattern.reshape(-1)
    two_halves = rhs[0].reshape(T, CORES, T).transpose(1, 0, 2)
    whole = lax.all_to_all(
        jnp.broadcast_to(two_halves[None], (chips, CORES, T, T)).reshape(columns, T, T), "col", 0, 0, tiled=True
    )
    inverse_other = swapped(inverse_blocks)
    tip_other = swapped(tip_coupling)
    lower_other = swapped(lower_coupling)
    upper_other = swapped(upper_coupling)
    inverses = (inverse_blocks, inverse_other)
    tips = (tip_coupling, tip_other)
    couplings = (lower_coupling, lower_other, upper_coupling, upper_other)
    height = fixed // columns
    near = rows // 4
    last = levels - 1
    for level in range(levels):
        stride = 2**level
        if level == 0:
            solved, tip, x = call(
                first_solve_kernel, [(chips, T, width), (fixed, T), (T, width)], 0, whole, *inverses, *tips
            )
        elif level < last:
            solved, tip = call(
                functools.partial(solve_kernel, level), [(chips, T, width), (fixed, T)], 0, whole, *inverses, *tips, tip
            )
        else:
            (solved,) = call(
                functools.partial(last_solve_kernel, level),
                [(chips, T + height, width)],
                0,
                whole,
                *inverses,
                *tips,
                tip,
            )
        whole_solved = exchanged(solved)
        down, up, *tip_message = call(
            functools.partial(couple_kernel, level),
            [(T, width), (T, width)] + [(near, height, width)] * (level == last),
            1,
            pattern,
            whole_solved,
            *couplings,
        )
        above = passed(down, "tm", lambda i: (i - stride) % rows)
        below = passed(up, "tm", lambda i: (i + stride) % rows)
        if level < last:
            message, x = call(advance_kernel, [(chips, T, width), (T, width)], 0, x, above, below)
            whole = exchanged(message)
    tip = lax.all_to_all(
        tip_message[0],
        "tm",
        0,
        0,
        axis_index_groups=[[near * q + i for i in range(near)] for q in range(rows // near)],
        tiled=True,
    ).sum(0)
    tip, above, below = lax.optimization_barrier((tip, above, below))
    keep, send = call(leave_kernel, [(T, T), (T, T)], 0, x, above, below)
    back = swapped(send)
    (reduced,) = call(place_kernel, [(1, T, width)], 0, keep, back)
    count = columns * (rows // near)
    tip_parts = lax.all_to_all(
        jnp.broadcast_to(tip[None], (count, height, width)),
        ("tm", "col"),
        0,
        0,
        axis_index_groups=[
            [(near * q + i) * columns + c for q in range(rows // near) for c in range(columns)] for i in range(near)
        ],
        tiled=True,
    )
    (tip_reduced,) = call(functools.partial(tip_kernel, chips), [(fixed, width)], 0, tip_rhs, tip_parts)
    return reduced, tip_reduced


def solution(mesh):
    return jax.shard_map(
        local,
        mesh=mesh,
        in_specs=(
            P("tm", "col", None),
            P(None, "tm", None, "col"),
            P(None, "tm", None, "col"),
            P(None, "tm", None, "col"),
            P(None, "tm", None, None, "col"),
            P(None, "tm", None, "col"),
            P(),
        ),
        out_specs=(P("tm", "col", None), P()),
        check_vma=False,
    )
```

```python
import functools

import jax
import jax.numpy as jnp
from jax import lax
from jax.experimental import pallas as pl
from jax.experimental.pallas import tpu as pltpu
from jax.sharding import PartitionSpec as P

T = 128
CORES = 2
VMEM = pl.BlockSpec(memory_space=pltpu.VMEM)
ANY = pl.BlockSpec(memory_space=pl.ANY)
SMEM = pl.BlockSpec(memory_space=pltpu.SMEM)


def own_core():
    return lax.rem(lax.axis_index("col"), CORES)


def lanes(half):
    return pl.ds(pl.multiple_of(half * T, T), T)


def halves(value):
    high = value.astype(jnp.bfloat16)
    return high, (value - high.astype(jnp.float32)).astype(jnp.bfloat16)


def mul(a, b, dims):
    return lax.dot_general(a, b, (dims, ((), ())), preferred_element_type=jnp.float32)


def product(left, right, dims=((1,), (0,))):
    rows = left.shape[0]
    left_high, left_low = halves(left)
    right_high, right_low = halves(right)
    both = mul(jnp.concatenate([left_high, left_low], axis=0), right_high, dims)
    return both[:rows] + both[rows:] + mul(left_high, right_low, dims)


def call(body, out_shapes, smem, *args, cost=None):
    return pl.pallas_call(
        body,
        out_shape=[jax.ShapeDtypeStruct(s, jnp.float32) for s in out_shapes],
        in_specs=[SMEM] * smem + [VMEM] * (len(args) - smem),
        out_specs=[VMEM] * len(out_shapes),
        cost_estimate=cost,
        compiler_params=pltpu.CompilerParams(vmem_limit_bytes=16 * 2**20),
    )(*args)


def column_blocks(ref, k):
    return jnp.concatenate([ref[CORES * k + c].T for c in range(CORES)], axis=1)


def message_kernel(rhs, out):
    for i in range(out.shape[0]):
        c = i % CORES
        out[i] = rhs[0, :, c * T : (c + 1) * T]


def own_columns(own, other, level, rows):
    return jnp.concatenate([own[level, 0, rows, :], other[level, 0, rows, :]], axis=1)


def in_order(out, index, value):
    core = own_core()
    out[(*index, lanes(core))] = value[:, :T]
    out[(*index, lanes(1 - core))] = value[:, T:]


def solve(x, level, own, other):
    parts, _, width = x.shape
    total = jnp.zeros((T, width), jnp.float32)
    for k in range(parts):
        total = total + product(x[k, :T, :], own_columns(own, other, level, pl.ds(k * width, width)))
    return total


def tip_term(level, tip_own, tip_other, solved):
    return product(jnp.concatenate([tip_own[level, 0], tip_other[level, 0]], axis=1), solved, ((1,), (1,)))


def first_solve_kernel(x, own, other, out, entered, solved):
    parts = out.shape[0]
    width = CORES * T
    total = jnp.zeros((T, width), jnp.float32)
    for k in range(parts):
        total = total + product(column_blocks(x, k), own_columns(own, other, 0, pl.ds(k * width, width)))
    solved[...] = total
    for k in range(parts):
        in_order(out, (k, slice(None)), total)
    chip = lax.div(lax.axis_index("col"), CORES)
    for c in range(CORES):
        entered[:, c * T : (c + 1) * T] = x[CORES * chip + c].T


def solve_kernel(level, x, own, other, tip_own, tip_other, before, out, tip):
    total = solve(x, level, own, other)
    for k in range(out.shape[0]):
        in_order(out, (k, slice(None)), total)
    tip[...] = tip_term(level, tip_own, tip_other, total) + (
        tip_term(0, tip_own, tip_other, before[...]) if level == 1 else before[...]
    )


def last_solve_kernel(level, x, own, other, tip_own, tip_other, tip_before, out):
    parts = out.shape[0]
    height = out.shape[1] - T
    total = solve(x, level, own, other)
    tip = tip_before[...] + tip_term(level, tip_own, tip_other, total)
    for k in range(parts):
        in_order(out, (k, slice(0, T)), total)
        for c in range(CORES):
            first = (CORES * k + c) * height
            out[k, pl.ds(T, height), c * T : (c + 1) * T] = tip[first : first + height]


def advance_kernel(x, above, below, out, x_out):
    now = x[...] - above[...] - below[...]
    x_out[...] = now
    for k in range(out.shape[0]):
        out[k] = now


def couple_kernel(level, pattern, s, low_own, low_other, up_own, up_other, down, up, *refs):
    *tip_out, low_here, up_here, semaphores = refs
    copies = [
        pltpu.make_async_copy(other.at[level, 0], here, semaphores.at[i])
        for i, (other, here) in enumerate(((low_other, low_here), (up_other, up_here)))
    ]
    for copy in copies:
        copy.start()
    core = own_core()
    column = lax.axis_index("col")
    beside = column + 1 - 2 * core
    parts = s.shape[0]
    width = CORES * T
    tiles = CORES * parts
    here = [[pattern[level, 0, which, 0, r] for r in range(tiles)] for which in range(2)]
    reach = []
    for which in range(2):
        reach.append(jnp.int32(0))
        for r in range(tiles):
            reach[which] = jnp.maximum(reach[which], jnp.where(here[which][r] > 0, jnp.abs(r - column), 0))

    def coupled(matrix, which, tile_column):
        total = jnp.zeros((T, T), jnp.float32)
        for k in range(parts):
            blocks = []
            for r in range(CORES * k, CORES * (k + 1)):
                mask = jnp.where(jnp.abs(r - tile_column) <= reach[which], 1.0, 0.0).astype(jnp.float32)
                blocks.append(matrix[pl.ds(r * T, T), :] * mask)
            total = total + product(s[k, :T, :], jnp.concatenate(blocks, axis=0))
        return total

    down[:, lanes(core)] = coupled(low_own.at[level, 0], 0, column)
    up[:, lanes(core)] = coupled(up_own.at[level, 0], 1, column)
    for which, (copy, matrix, out) in enumerate(zip(copies, (low_here, up_here), (down, up))):
        copy.wait()
        out[:, lanes(1 - core)] = coupled(matrix, which, beside)
    if tip_out:
        count, height, _ = tip_out[0].shape
        tip = sum(s[k, pl.ds(T, height), :] for k in range(parts))
        for i in range(count):
            tip_out[0][i] = tip


def leave_kernel(x, above, below, keep, send):
    core = own_core()
    for half, out in ((core, keep), (1 - core, send)):
        out[...] = x[:, lanes(half)] - above[:, lanes(half)] - below[:, lanes(half)]


def place_kernel(keep, received, out):
    core = own_core()
    out[0, :, lanes(core)] = keep[...].T
    out[0, :, lanes(1 - core)] = received[...].T


def tip_kernel(chips, tip_rhs, parts, out):
    height = parts.shape[1]
    count = parts.shape[0] // (CORES * chips)
    for chip in range(chips):
        for core in range(CORES):
            place = CORES * chip + core
            total = sum(parts[CORES * chips * q + place] for q in range(count))
            columns = pl.ds(core * T, T)
            for c in range(CORES):
                rows = pl.ds((CORES * chip + c) * height, height)
                out[rows, columns] = tip_rhs[rows, columns] - total[:, c * T : (c + 1) * T]


def passed(block, axis, target):
    return lax.ppermute(block, axis, [(i, target(i)) for i in range(lax.axis_size(axis))])


def local(rhs, inverse_blocks, lower_coupling, upper_coupling, tile_pattern, tip_coupling, tip_rhs):
    levels = inverse_blocks.shape[0]
    fixed = tip_rhs.shape[0]
    columns, rows = lax.axis_size("col"), lax.axis_size("tm")
    chips = columns // CORES
    width = CORES * T
    core = own_core()
    same_core = [[c + CORES * k for k in range(chips)] for c in range(CORES)]

    def swapped(block):
        return passed(block, "col", lambda i: i ^ 1)

    def exchanged(block):
        return lax.all_to_all(block, "col", 0, 0, axis_index_groups=same_core, tiled=True)

    pattern = tile_pattern.transpose(0, 1, 2, 4, 3)
    (message,) = call(message_kernel, [(columns, T, T)], 0, rhs)
    whole = lax.all_to_all(message, "col", 0, 0, tiled=True)
    inverse_other = swapped(inverse_blocks)
    lower_other = swapped(lower_coupling)
    upper_other = swapped(upper_coupling)
    inverses = (inverse_blocks, inverse_other)
    couplings = (lower_coupling, lower_other, upper_coupling, upper_other)
    height = fixed // columns
    near = rows // 4
    last = levels - 1
    for level in range(levels):
        stride = 2**level
        if level == 0:
            solved, x, tip = call(
                first_solve_kernel, [(chips, T, width), (T, width), (T, width)], 0, whole, *inverses
            )
            solved, *couplings = lax.optimization_barrier((solved, *couplings))
        elif level < last:
            solved, tip = call(
                functools.partial(solve_kernel, level),
                [(chips, T, width), (fixed, T)],
                0,
                whole,
                *inverses,
                tip_coupling,
                tip_other,
                tip,
            )
        else:
            (solved,) = call(
                functools.partial(last_solve_kernel, level),
                [(chips, T + height, width)],
                0,
                whole,
                *inverses,
                tip_coupling,
                tip_other,
                tip,
            )
        whole_solved = exchanged(solved)
        down, up, *tip_message = pl.pallas_call(
            functools.partial(couple_kernel, level),
            out_shape=[
                jax.ShapeDtypeStruct(shape, jnp.float32)
                for shape in [(T, width), (T, width)] + [(near, height, width)] * (level == last)
            ],
            in_specs=[SMEM, VMEM, VMEM, ANY, VMEM, ANY],
            out_specs=[VMEM] * (2 + (level == last)),
            scratch_shapes=[
                pltpu.VMEM((chips * width, T), jnp.float32),
                pltpu.VMEM((chips * width, T), jnp.float32),
                pltpu.SemaphoreType.DMA((2,)),
            ],
            compiler_params=pltpu.CompilerParams(vmem_limit_bytes=16 * 2**20),
        )(pattern, whole_solved, *couplings)
        if level == 0:
            down, tip_sent = lax.optimization_barrier((down, tip_coupling))
            tip_other = swapped(tip_sent)
        above = passed(down, "tm", lambda i: (i - stride) % rows)
        below = passed(up, "tm", lambda i: (i + stride) % rows)
        if level < last:
            message, x = call(advance_kernel, [(chips, T, width), (T, width)], 0, x, above, below)
            message, tip_other = lax.optimization_barrier((message, tip_other))
            whole = exchanged(message)
    tip = lax.all_to_all(
        tip_message[0],
        "tm",
        0,
        0,
        axis_index_groups=[[near * q + i for i in range(near)] for q in range(rows // near)],
        tiled=True,
    ).sum(0)
    keep, send = call(leave_kernel, [(T, T), (T, T)], 0, x, above, below, cost=pl.CostEstimate(flops=2 * 10**10, bytes_accessed=0, transcendentals=0))
    back = swapped(send)
    (reduced,) = call(place_kernel, [(1, T, width)], 0, keep, back)
    count = columns * (rows // near)
    tip_parts = lax.all_to_all(
        jnp.broadcast_to(tip[None], (count, height, width)),
        ("tm", "col"),
        0,
        0,
        axis_index_groups=[
            [(near * q + i) * columns + c for q in range(rows // near) for c in range(columns)] for i in range(near)
        ],
        tiled=True,
    )
    (tip_reduced,) = call(functools.partial(tip_kernel, chips), [(fixed, width)], 0, tip_rhs, tip_parts)
    return reduced, tip_reduced


def solution(mesh):
    return jax.shard_map(
        local,
        mesh=mesh,
        in_specs=(
            P("tm", "col", None),
            P(None, "tm", None, "col"),
            P(None, "tm", None, "col"),
            P(None, "tm", None, "col"),
            P(None, "tm", None, None, "col"),
            P(None, "tm", None, "col"),
            P(),
        ),
        out_specs=(P("tm", "col", None), P()),
        check_vma=False,
    )
```

```python
import functools

import jax
import jax.numpy as jnp
from jax import lax
from jax.experimental import pallas as pl
from jax.experimental.pallas import tpu as pltpu
from jax.sharding import PartitionSpec as P

T = 128
CORES = 2
VMEM = pl.BlockSpec(memory_space=pltpu.VMEM)
SMEM = pl.BlockSpec(memory_space=pltpu.SMEM)


def own_core():
    return lax.rem(lax.axis_index("col"), CORES)


def lanes(half):
    return pl.ds(pl.multiple_of(half * T, T), T)


def halves(value):
    high = value.astype(jnp.bfloat16)
    return high, (value - high.astype(jnp.float32)).astype(jnp.bfloat16)


def mul(a, b, dims):
    return lax.dot_general(a, b, (dims, ((), ())), preferred_element_type=jnp.float32)


def product(left, right, dims=((1,), (0,))):
    rows = left.shape[0]
    left_high, left_low = halves(left)
    right_high, right_low = halves(right)
    both = mul(jnp.concatenate([left_high, left_low], axis=0), right_high, dims)
    return both[:rows] + both[rows:] + mul(left_high, right_low, dims)


def call(body, out_shapes, smem, *args, cost=None):
    return pl.pallas_call(
        body,
        out_shape=[jax.ShapeDtypeStruct(s, jnp.float32) for s in out_shapes],
        in_specs=[SMEM] * smem + [VMEM] * (len(args) - smem),
        out_specs=[VMEM] * len(out_shapes),
        cost_estimate=cost
        or pl.CostEstimate(flops=10**9, bytes_accessed=sum(a.size * 4 for a in args), transcendentals=0),
        compiler_params=pltpu.CompilerParams(vmem_limit_bytes=16 * 2**20),
    )(*args)


def column_blocks(ref, k):
    return jnp.concatenate([ref[CORES * k + c].T for c in range(CORES)], axis=1)


def message_kernel(rhs, out):
    for i in range(out.shape[0]):
        c = i % CORES
        out[i] = rhs[0, :, c * T : (c + 1) * T]


def own_columns(own, other, level, rows):
    return jnp.concatenate([own[level, 0, rows, :], other[level, 0, rows, :]], axis=1)


def in_order(out, index, value):
    core = own_core()
    out[(*index, lanes(core))] = value[:, :T]
    out[(*index, lanes(1 - core))] = value[:, T:]


def solve(x, level, own, other):
    parts, _, width = x.shape
    total = jnp.zeros((T, width), jnp.float32)
    for k in range(parts):
        total = total + product(x[k, :T, :], own_columns(own, other, level, pl.ds(k * width, width)))
    return total


def tip_term(level, tip_own, tip_other, solved):
    return product(jnp.concatenate([tip_own[level, 0], tip_other[level, 0]], axis=1), solved, ((1,), (1,)))


def first_solve_kernel(x, own, other, out, entered, solved):
    parts = out.shape[0]
    width = CORES * T
    total = jnp.zeros((T, width), jnp.float32)
    for k in range(parts):
        total = total + product(column_blocks(x, k), own_columns(own, other, 0, pl.ds(k * width, width)))
    solved[...] = total
    for k in range(parts):
        in_order(out, (k, slice(None)), total)
    chip = lax.div(lax.axis_index("col"), CORES)
    for c in range(CORES):
        entered[:, c * T : (c + 1) * T] = x[CORES * chip + c].T


def solve_kernel(level, x, own, other, out, solved):
    total = solve(x, level, own, other)
    solved[...] = total
    for k in range(out.shape[0]):
        in_order(out, (k, slice(None)), total)


def last_solve_kernel(level, x, own, other, tip_own, tip_other, *refs):
    *earlier, out = refs
    parts = out.shape[0]
    height = out.shape[1] - T
    total = solve(x, level, own, other)
    tip = tip_term(level, tip_own, tip_other, total)
    for before, solved in enumerate(earlier):
        tip = tip + tip_term(before, tip_own, tip_other, solved[...])
    for k in range(parts):
        in_order(out, (k, slice(0, T)), total)
        for c in range(CORES):
            first = (CORES * k + c) * height
            out[k, pl.ds(T, height), c * T : (c + 1) * T] = tip[first : first + height]


def advance_kernel(x, above, below, out, x_out):
    now = x[...] - above[...] - below[...]
    x_out[...] = now
    for k in range(out.shape[0]):
        out[k] = now


def couple_kernel(level, pattern, s, low_own, low_other, up_own, up_other, down, up, *tip_out):
    core = own_core()
    column = lax.axis_index("col")
    beside = column + 1 - 2 * core
    parts = s.shape[0]
    width = CORES * T
    tiles = CORES * parts
    here = [[pattern[level, 0, which, 0, r] for r in range(tiles)] for which in range(2)]
    reach = []
    for which in range(2):
        reach.append(jnp.int32(0))
        for r in range(tiles):
            reach[which] = jnp.maximum(reach[which], jnp.where(here[which][r] > 0, jnp.abs(r - column), 0))

    def coupled(low, high, tile_column, half):
        total = jnp.zeros((T, 2 * T), jnp.float32)
        for k in range(parts):
            blocks = []
            for r in range(CORES * k, CORES * (k + 1)):
                near = jnp.abs(r - tile_column)
                blocks.append(
                    jnp.concatenate(
                        [
                            matrix[level, 0, pl.ds(r * T, T), :]
                            * jnp.where(near <= reach[which], 1.0, 0.0).astype(jnp.float32)
                            for which, matrix in enumerate((low, high))
                        ],
                        axis=1,
                    )
                )
            total = total + product(s[k, :T, :], jnp.concatenate(blocks, axis=0))
        down[:, lanes(half)] = total[:, :T]
        up[:, lanes(half)] = total[:, T:]

    coupled(low_own, up_own, column, core)
    coupled(low_other, up_other, beside, 1 - core)
    if tip_out:
        count, height, _ = tip_out[0].shape
        tip = sum(s[k, pl.ds(T, height), :] for k in range(parts))
        for i in range(count):
            tip_out[0][i] = tip


def leave_kernel(x, above, below, keep, send):
    core = own_core()
    for half, out in ((core, keep), (1 - core, send)):
        out[...] = x[:, lanes(half)] - above[:, lanes(half)] - below[:, lanes(half)]


def place_kernel(keep, received, out):
    core = own_core()
    out[0, :, lanes(core)] = keep[...].T
    out[0, :, lanes(1 - core)] = received[...].T


def tip_kernel(chips, tip_rhs, parts, out):
    height = parts.shape[1]
    count = parts.shape[0] // (CORES * chips)
    for chip in range(chips):
        for core in range(CORES):
            place = CORES * chip + core
            total = sum(parts[CORES * chips * q + place] for q in range(count))
            columns = pl.ds(core * T, T)
            for c in range(CORES):
                rows = pl.ds((CORES * chip + c) * height, height)
                out[rows, columns] = tip_rhs[rows, columns] - total[:, c * T : (c + 1) * T]


def passed(block, axis, target):
    return lax.ppermute(block, axis, [(i, target(i)) for i in range(lax.axis_size(axis))])


def local(rhs, inverse_blocks, lower_coupling, upper_coupling, tile_pattern, tip_coupling, tip_rhs):
    levels = inverse_blocks.shape[0]
    fixed = tip_rhs.shape[0]
    columns, rows = lax.axis_size("col"), lax.axis_size("tm")
    chips = columns // CORES
    width = CORES * T
    core = own_core()
    same_core = [[c + CORES * k for k in range(chips)] for c in range(CORES)]

    def swapped(block):
        return passed(block, "col", lambda i: i ^ 1)

    def exchanged(block):
        return lax.all_to_all(block, "col", 0, 0, axis_index_groups=same_core, tiled=True)

    pattern = tile_pattern.transpose(0, 1, 2, 4, 3)
    (message,) = call(message_kernel, [(columns, T, T)], 0, rhs)
    whole = lax.all_to_all(message, "col", 0, 0, tiled=True)
    inverse_other = swapped(inverse_blocks)
    lower_other = swapped(lower_coupling)
    upper_other = swapped(upper_coupling)
    inverses = (inverse_blocks, inverse_other)
    couplings = (lower_coupling, lower_other, upper_coupling, upper_other)
    height = fixed // columns
    near = rows // 4
    last = levels - 1
    for level in range(levels):
        stride = 2**level
        if level == 0:
            solved, x, kept = call(
                first_solve_kernel, [(chips, T, width), (T, width), (T, width)], 0, whole, *inverses
            )
            earlier = [kept]
            solved, *couplings = lax.optimization_barrier((solved, *couplings))
        elif level < last:
            solved, kept = call(
                functools.partial(solve_kernel, level), [(chips, T, width), (T, width)], 0, whole, *inverses
            )
            earlier.append(kept)
        else:
            (solved,) = call(
                functools.partial(last_solve_kernel, level),
                [(chips, T + height, width)],
                0,
                whole,
                *inverses,
                tip_coupling,
                tip_other,
                *earlier,
            )
        whole_solved = exchanged(solved)
        down, up, *tip_message = call(
            functools.partial(couple_kernel, level),
            [(T, width), (T, width)] + [(near, height, width)] * (level == last),
            1,
            pattern,
            whole_solved,
            *couplings,
        )
        if level == last - 1:
            down, tip_sent = lax.optimization_barrier((down, tip_coupling))
            tip_other = swapped(tip_sent)
        above = passed(down, "tm", lambda i: (i - stride) % rows)
        below = passed(up, "tm", lambda i: (i + stride) % rows)
        if level < last:
            message, x = call(advance_kernel, [(chips, T, width), (T, width)], 0, x, above, below)
            if level == last - 1:
                message, tip_other = lax.optimization_barrier((message, tip_other))
            whole = exchanged(message)
    tip = lax.all_to_all(
        tip_message[0],
        "tm",
        0,
        0,
        axis_index_groups=[[near * q + i for i in range(near)] for q in range(rows // near)],
        tiled=True,
    ).sum(0)
    keep, send = call(leave_kernel, [(T, T), (T, T)], 0, x, above, below, cost=pl.CostEstimate(flops=2 * 10**10, bytes_accessed=0, transcendentals=0))
    back = swapped(send)
    (reduced,) = call(place_kernel, [(1, T, width)], 0, keep, back)
    count = columns * (rows // near)
    tip_parts = lax.all_to_all(
        jnp.broadcast_to(tip[None], (count, height, width)),
        ("tm", "col"),
        0,
        0,
        axis_index_groups=[
            [(near * q + i) * columns + c for q in range(rows // near) for c in range(columns)] for i in range(near)
        ],
        tiled=True,
    )
    (tip_reduced,) = call(functools.partial(tip_kernel, chips), [(fixed, width)], 0, tip_rhs, tip_parts)
    return reduced, tip_reduced


def solution(mesh):
    return jax.shard_map(
        local,
        mesh=mesh,
        in_specs=(
            P("tm", "col", None),
            P(None, "tm", None, "col"),
            P(None, "tm", None, "col"),
            P(None, "tm", None, "col"),
            P(None, "tm", None, None, "col"),
            P(None, "tm", None, "col"),
            P(),
        ),
        out_specs=(P("tm", "col", None), P()),
        check_vma=False,
    )
```

```python
import functools

import jax
import jax.numpy as jnp
from jax import lax
from jax.experimental import pallas as pl
from jax.experimental.pallas import tpu as pltpu
from jax.sharding import PartitionSpec as P

T = 128
CORES = 2
VMEM = pl.BlockSpec(memory_space=pltpu.VMEM)
SMEM = pl.BlockSpec(memory_space=pltpu.SMEM)


def own_core():
    return lax.rem(lax.axis_index("col"), CORES)


def lanes(half):
    return pl.ds(pl.multiple_of(half * T, T), T)


def halves(value):
    high = value.astype(jnp.bfloat16)
    return high, (value - high.astype(jnp.float32)).astype(jnp.bfloat16)


def mul(a, b, dims):
    return lax.dot_general(a, b, (dims, ((), ())), preferred_element_type=jnp.float32)


def product(left, right, dims=((1,), (0,))):
    rows = left.shape[0]
    left_high, left_low = halves(left)
    right_high, right_low = halves(right)
    both = mul(jnp.concatenate([left_high, left_low], axis=0), right_high, dims)
    return both[:rows] + both[rows:] + mul(left_high, right_low, dims)


def call(body, out_shapes, smem, *args, cost=None):
    return pl.pallas_call(
        body,
        out_shape=[jax.ShapeDtypeStruct(s, jnp.float32) for s in out_shapes],
        in_specs=[SMEM] * smem + [VMEM] * (len(args) - smem),
        out_specs=[VMEM] * len(out_shapes),
        cost_estimate=cost
        or pl.CostEstimate(flops=10**9, bytes_accessed=sum(a.size * 4 for a in args), transcendentals=0),
        compiler_params=pltpu.CompilerParams(vmem_limit_bytes=16 * 2**20),
    )(*args)


def column_blocks(ref, k):
    return jnp.concatenate([ref[CORES * k + c].T for c in range(CORES)], axis=1)


def message_kernel(rhs, out):
    for i in range(out.shape[0]):
        c = i % CORES
        out[i] = rhs[0, :, c * T : (c + 1) * T]


def own_columns(own, other, level, rows):
    return jnp.concatenate([own[level, 0, rows, :], other[level, 0, rows, :]], axis=1)


def in_order(out, index, value):
    core = own_core()
    out[(*index, lanes(core))] = value[:, :T]
    out[(*index, lanes(1 - core))] = value[:, T:]


def solve(x, level, own, other):
    parts, _, width = x.shape
    total = jnp.zeros((T, width), jnp.float32)
    for k in range(parts):
        total = total + product(x[k, :T, :], own_columns(own, other, level, pl.ds(k * width, width)))
    return total


def tip_term(level, tip_own, tip_other, solved):
    return product(jnp.concatenate([tip_own[level, 0], tip_other[level, 0]], axis=1), solved, ((1,), (1,)))


def first_solve_kernel(x, own, other, out, entered, solved):
    parts = out.shape[0]
    width = CORES * T
    total = jnp.zeros((T, width), jnp.float32)
    for k in range(parts):
        total = total + product(column_blocks(x, k), own_columns(own, other, 0, pl.ds(k * width, width)))
    solved[...] = total
    for k in range(parts):
        in_order(out, (k, slice(None)), total)
    chip = lax.div(lax.axis_index("col"), CORES)
    for c in range(CORES):
        entered[:, c * T : (c + 1) * T] = x[CORES * chip + c].T


def solve_kernel(level, x, own, other, out, solved):
    total = solve(x, level, own, other)
    solved[...] = total
    for k in range(out.shape[0]):
        in_order(out, (k, slice(None)), total)


def last_solve_kernel(level, x, own, other, tip_own, tip_other, *refs):
    *earlier, out = refs
    parts = out.shape[0]
    height = out.shape[1] - T
    total = solve(x, level, own, other)
    tip = tip_term(level, tip_own, tip_other, total)
    for before, solved in enumerate(earlier):
        tip = tip + tip_term(before, tip_own, tip_other, solved[...])
    for k in range(parts):
        in_order(out, (k, slice(0, T)), total)
        for c in range(CORES):
            first = (CORES * k + c) * height
            out[k, pl.ds(T, height), c * T : (c + 1) * T] = tip[first : first + height]


def advance_kernel(x, above, below, out, x_out):
    now = x[...] - above[...] - below[...]
    x_out[...] = now
    for k in range(out.shape[0]):
        out[k] = now


def first_couple_kernel(pattern, s, low_own, low_other, up_own, up_other, down, up, masks):
    core = own_core()
    column = lax.axis_index("col")
    tiles = pattern.shape[4]
    for level in range(pattern.shape[0]):
        for which in range(2):
            reach = jnp.int32(0)
            for r in range(tiles):
                reach = jnp.maximum(
                    reach, jnp.where(pattern[level, 0, which, 0, r] > 0, jnp.abs(r - column), 0)
                )
            for side, tile_column in enumerate((column, column + 1 - 2 * core)):
                distance = jnp.abs(lax.broadcasted_iota(jnp.int32, (tiles, T), 0) - tile_column)
                masks[level, side, :, which * T : (which + 1) * T] = (distance <= reach).astype(jnp.float32)
    couple_kernel(0, masks, s, low_own, low_other, up_own, up_other, down, up)


def couple_kernel(level, masks, s, low_own, low_other, up_own, up_other, down, up, *tip_out):
    core = own_core()
    parts = s.shape[0]

    def coupled(low, high, side, half):
        total = jnp.zeros((T, 2 * T), jnp.float32)
        for k in range(parts):
            blocks = []
            for r in range(CORES * k, CORES * (k + 1)):
                columns = [matrix[level, 0, pl.ds(r * T, T), :] for matrix in (low, high)]
                blocks.append(jnp.concatenate(columns, axis=1) * masks[level, side, r : r + 1, :])
            total = total + product(s[k, :T, :], jnp.concatenate(blocks, axis=0))
        down[:, lanes(half)] = total[:, :T]
        up[:, lanes(half)] = total[:, T:]

    coupled(low_own, up_own, 0, core)
    coupled(low_other, up_other, 1, 1 - core)
    if tip_out:
        count, height, _ = tip_out[0].shape
        tip = sum(s[k, pl.ds(T, height), :] for k in range(parts))
        for i in range(count):
            tip_out[0][i] = tip


def leave_kernel(x, above, below, keep, send):
    core = own_core()
    for half, out in ((core, keep), (1 - core, send)):
        out[...] = x[:, lanes(half)] - above[:, lanes(half)] - below[:, lanes(half)]


def place_kernel(keep, received, out):
    core = own_core()
    out[0, :, lanes(core)] = keep[...].T
    out[0, :, lanes(1 - core)] = received[...].T


def tip_kernel(chips, tip_rhs, parts, out):
    height = parts.shape[1]
    count = parts.shape[0] // (CORES * chips)
    for chip in range(chips):
        for core in range(CORES):
            place = CORES * chip + core
            total = sum(parts[CORES * chips * q + place] for q in range(count))
            columns = pl.ds(core * T, T)
            for c in range(CORES):
                rows = pl.ds((CORES * chip + c) * height, height)
                out[rows, columns] = tip_rhs[rows, columns] - total[:, c * T : (c + 1) * T]


def passed(block, axis, target):
    return lax.ppermute(block, axis, [(i, target(i)) for i in range(lax.axis_size(axis))])


def local(rhs, inverse_blocks, lower_coupling, upper_coupling, tile_pattern, tip_coupling, tip_rhs):
    levels = inverse_blocks.shape[0]
    fixed = tip_rhs.shape[0]
    columns, rows = lax.axis_size("col"), lax.axis_size("tm")
    chips = columns // CORES
    width = CORES * T
    core = own_core()
    same_core = [[c + CORES * k for k in range(chips)] for c in range(CORES)]

    def swapped(block):
        return passed(block, "col", lambda i: i ^ 1)

    def exchanged(block):
        return lax.all_to_all(block, "col", 0, 0, axis_index_groups=same_core, tiled=True)

    pattern = tile_pattern.transpose(0, 1, 2, 4, 3)
    (message,) = call(message_kernel, [(columns, T, T)], 0, rhs)
    whole = lax.all_to_all(message, "col", 0, 0, tiled=True)
    inverse_other = swapped(inverse_blocks)
    lower_other = swapped(lower_coupling)
    upper_other = swapped(upper_coupling)
    inverses = (inverse_blocks, inverse_other)
    couplings = (lower_coupling, lower_other, upper_coupling, upper_other)
    height = fixed // columns
    near = rows // 4
    last = levels - 1
    for level in range(levels):
        stride = 2**level
        if level == 0:
            solved, x, kept = call(
                first_solve_kernel, [(chips, T, width), (T, width), (T, width)], 0, whole, *inverses
            )
            earlier = [kept]
            solved, *couplings = lax.optimization_barrier((solved, *couplings))
        elif level < last:
            solved, kept = call(
                functools.partial(solve_kernel, level), [(chips, T, width), (T, width)], 0, whole, *inverses
            )
            earlier.append(kept)
        else:
            (solved,) = call(
                functools.partial(last_solve_kernel, level),
                [(chips, T + height, width)],
                0,
                whole,
                *inverses,
                tip_coupling,
                tip_other,
                *earlier,
            )
        whole_solved = exchanged(solved)
        if level == 0:
            down, up, masks = call(
                first_couple_kernel,
                [(T, width), (T, width), (levels, CORES, columns, width)],
                1,
                pattern,
                whole_solved,
                *couplings,
            )
        else:
            down, up, *tip_message = call(
                functools.partial(couple_kernel, level),
                [(T, width), (T, width)] + [(near, height, width)] * (level == last),
                0,
                masks,
                whole_solved,
                *couplings,
            )
        if level == last - 1:
            down, tip_sent = lax.optimization_barrier((down, tip_coupling))
            tip_other = swapped(tip_sent)
        above = passed(down, "tm", lambda i: (i - stride) % rows)
        below = passed(up, "tm", lambda i: (i + stride) % rows)
        if level < last:
            message, x = call(advance_kernel, [(chips, T, width), (T, width)], 0, x, above, below)
            if level == last - 1:
                message, tip_other = lax.optimization_barrier((message, tip_other))
            whole = exchanged(message)
    tip = lax.all_to_all(
        tip_message[0],
        "tm",
        0,
        0,
        axis_index_groups=[[near * q + i for i in range(near)] for q in range(rows // near)],
        tiled=True,
    ).sum(0)
    keep, send = call(leave_kernel, [(T, T), (T, T)], 0, x, above, below, cost=pl.CostEstimate(flops=2 * 10**10, bytes_accessed=0, transcendentals=0))
    back = swapped(send)
    (reduced,) = call(place_kernel, [(1, T, width)], 0, keep, back)
    count = columns * (rows // near)
    tip_parts = lax.all_to_all(
        jnp.broadcast_to(tip[None], (count, height, width)),
        ("tm", "col"),
        0,
        0,
        axis_index_groups=[
            [(near * q + i) * columns + c for q in range(rows // near) for c in range(columns)] for i in range(near)
        ],
        tiled=True,
    )
    (tip_reduced,) = call(functools.partial(tip_kernel, chips), [(fixed, width)], 0, tip_rhs, tip_parts)
    return reduced, tip_reduced


def solution(mesh):
    return jax.shard_map(
        local,
        mesh=mesh,
        in_specs=(
            P("tm", "col", None),
            P(None, "tm", None, "col"),
            P(None, "tm", None, "col"),
            P(None, "tm", None, "col"),
            P(None, "tm", None, None, "col"),
            P(None, "tm", None, "col"),
            P(),
        ),
        out_specs=(P("tm", "col", None), P()),
        check_vma=False,
    )
```

```python
import functools

import jax
import jax.numpy as jnp
from jax import lax
from jax.experimental import pallas as pl
from jax.experimental.pallas import tpu as pltpu
from jax.sharding import PartitionSpec as P

T = 128
CORES = 2
VMEM = pl.BlockSpec(memory_space=pltpu.VMEM)
SMEM = pl.BlockSpec(memory_space=pltpu.SMEM)


def own_core():
    return lax.rem(lax.axis_index("col"), CORES)


def lanes(half):
    return pl.ds(pl.multiple_of(half * T, T), T)


def halves(value):
    high = value.astype(jnp.bfloat16)
    return high, (value - high.astype(jnp.float32)).astype(jnp.bfloat16)


def mul(a, b, dims):
    return lax.dot_general(a, b, (dims, ((), ())), preferred_element_type=jnp.float32)


def product(left, right, dims=((1,), (0,))):
    rows = left.shape[0]
    left_high, left_low = halves(left)
    right_high, right_low = halves(right)
    both = mul(jnp.concatenate([left_high, left_low], axis=0), right_high, dims)
    return both[:rows] + both[rows:] + mul(left_high, right_low, dims)


def call(body, out_shapes, smem, *args, cost=None):
    return pl.pallas_call(
        body,
        out_shape=[jax.ShapeDtypeStruct(s, jnp.float32) for s in out_shapes],
        in_specs=[SMEM] * smem + [VMEM] * (len(args) - smem),
        out_specs=[VMEM] * len(out_shapes),
        cost_estimate=cost
        or pl.CostEstimate(flops=10**9, bytes_accessed=sum(a.size * 4 for a in args), transcendentals=0),
        compiler_params=pltpu.CompilerParams(vmem_limit_bytes=16 * 2**20),
    )(*args)


def column_blocks(ref, k):
    return jnp.concatenate([ref[CORES * k + c].T for c in range(CORES)], axis=1)


def message_kernel(rhs, out):
    for i in range(out.shape[0]):
        c = i % CORES
        out[i] = rhs[0, :, c * T : (c + 1) * T]


def own_columns(own, other, level, rows):
    return jnp.concatenate([own[level, 0, rows, :], other[level, 0, rows, :]], axis=1)


def in_order(out, index, value):
    core = own_core()
    out[(*index, lanes(core))] = value[:, :T]
    out[(*index, lanes(1 - core))] = value[:, T:]


def solve(x, level, own, other):
    parts, _, width = x.shape
    total = jnp.zeros((T, width), jnp.float32)
    for k in range(parts):
        total = total + product(x[k, :T, :], own_columns(own, other, level, pl.ds(k * width, width)))
    return total


def first_solve_kernel(x, own, other, out, entered, solved):
    parts = out.shape[0]
    width = CORES * T
    total = jnp.zeros((T, width), jnp.float32)
    for k in range(parts):
        total = total + product(column_blocks(x, k), own_columns(own, other, 0, pl.ds(k * width, width)))
    solved[...] = total
    for k in range(parts):
        in_order(out, (k, slice(None)), total)
    chip = lax.div(lax.axis_index("col"), CORES)
    for c in range(CORES):
        entered[:, c * T : (c + 1) * T] = x[CORES * chip + c].T


def solve_kernel(level, x, own, other, out, solved):
    total = solve(x, level, own, other)
    solved[...] = total
    for k in range(out.shape[0]):
        in_order(out, (k, slice(None)), total)


def last_solve_kernel(level, x, own, other, tip_own, tip_other, *refs):
    *earlier, out = refs
    parts = out.shape[0]
    height = out.shape[1] - T
    total = solve(x, level, own, other)
    fixed = [ref[i, 0] for i in range(level + 1) for ref in (tip_own, tip_other)]
    every = [solved[...] for solved in earlier] + [total]
    tip = product(jnp.concatenate(fixed, axis=1), jnp.concatenate(every, axis=1), ((1,), (1,)))
    for k in range(parts):
        in_order(out, (k, slice(0, T)), total)
        for c in range(CORES):
            first = (CORES * k + c) * height
            out[k, pl.ds(T, height), c * T : (c + 1) * T] = tip[first : first + height]


def advance_kernel(x, above, below, out, x_out):
    now = x[...] - above[...] - below[...]
    x_out[...] = now
    for k in range(out.shape[0]):
        out[k] = now


def first_couple_kernel(pattern, s, low_own, low_other, up_own, up_other, down, up, masks):
    core = own_core()
    column = lax.axis_index("col")
    tiles = pattern.shape[4]
    for level in range(pattern.shape[0]):
        for which in range(2):
            reach = jnp.int32(0)
            for r in range(tiles):
                reach = jnp.maximum(
                    reach, jnp.where(pattern[level, 0, which, 0, r] > 0, jnp.abs(r - column), 0)
                )
            for side, tile_column in enumerate((column, column + 1 - 2 * core)):
                distance = jnp.abs(lax.broadcasted_iota(jnp.int32, (tiles, T), 0) - tile_column)
                masks[level, side, :, which * T : (which + 1) * T] = (distance <= reach).astype(jnp.float32)
    couple_kernel(0, masks, s, low_own, low_other, up_own, up_other, down, up)


def couple_kernel(level, masks, s, low_own, low_other, up_own, up_other, down, up, *tip_out):
    core = own_core()
    parts = s.shape[0]

    def coupled(low, high, side, half):
        total = jnp.zeros((T, 2 * T), jnp.float32)
        for k in range(parts):
            blocks = []
            for r in range(CORES * k, CORES * (k + 1)):
                columns = [matrix[level, 0, pl.ds(r * T, T), :] for matrix in (low, high)]
                blocks.append(jnp.concatenate(columns, axis=1) * masks[level, side, r : r + 1, :])
            total = total + product(s[k, :T, :], jnp.concatenate(blocks, axis=0))
        down[:, lanes(half)] = total[:, :T]
        up[:, lanes(half)] = total[:, T:]

    coupled(low_own, up_own, 0, core)
    coupled(low_other, up_other, 1, 1 - core)
    if tip_out:
        count, height, _ = tip_out[0].shape
        tip = sum(s[k, pl.ds(T, height), :] for k in range(parts))
        for i in range(count):
            tip_out[0][i] = tip


def leave_kernel(x, above, below, keep, send):
    core = own_core()
    for half, out in ((core, keep), (1 - core, send)):
        out[...] = x[:, lanes(half)] - above[:, lanes(half)] - below[:, lanes(half)]


def place_kernel(keep, received, out):
    core = own_core()
    out[0, :, lanes(core)] = keep[...].T
    out[0, :, lanes(1 - core)] = received[...].T


def tip_kernel(chips, tip_rhs, parts, out):
    height = parts.shape[1]
    count = parts.shape[0] // (CORES * chips)
    for chip in range(chips):
        for core in range(CORES):
            place = CORES * chip + core
            total = sum(parts[CORES * chips * q + place] for q in range(count))
            columns = pl.ds(core * T, T)
            for c in range(CORES):
                rows = pl.ds((CORES * chip + c) * height, height)
                out[rows, columns] = tip_rhs[rows, columns] - total[:, c * T : (c + 1) * T]


def passed(block, axis, target):
    return lax.ppermute(block, axis, [(i, target(i)) for i in range(lax.axis_size(axis))])


def local(rhs, inverse_blocks, lower_coupling, upper_coupling, tile_pattern, tip_coupling, tip_rhs):
    levels = inverse_blocks.shape[0]
    fixed = tip_rhs.shape[0]
    columns, rows = lax.axis_size("col"), lax.axis_size("tm")
    chips = columns // CORES
    width = CORES * T
    core = own_core()
    same_core = [[c + CORES * k for k in range(chips)] for c in range(CORES)]

    def swapped(block):
        return passed(block, "col", lambda i: i ^ 1)

    def exchanged(block):
        return lax.all_to_all(block, "col", 0, 0, axis_index_groups=same_core, tiled=True)

    pattern = tile_pattern.transpose(0, 1, 2, 4, 3)
    (message,) = call(message_kernel, [(columns, T, T)], 0, rhs)
    whole = lax.all_to_all(message, "col", 0, 0, tiled=True)
    inverse_other = swapped(inverse_blocks)
    lower_other = swapped(lower_coupling)
    upper_other = swapped(upper_coupling)
    inverses = (inverse_blocks, inverse_other)
    couplings = (lower_coupling, lower_other, upper_coupling, upper_other)
    height = fixed // columns
    near = rows // 4
    last = levels - 1
    for level in range(levels):
        stride = 2**level
        if level == 0:
            solved, x, kept = call(
                first_solve_kernel, [(chips, T, width), (T, width), (T, width)], 0, whole, *inverses
            )
            earlier = [kept]
            solved, *couplings = lax.optimization_barrier((solved, *couplings))
        elif level < last:
            solved, kept = call(
                functools.partial(solve_kernel, level), [(chips, T, width), (T, width)], 0, whole, *inverses
            )
            earlier.append(kept)
        else:
            (solved,) = call(
                functools.partial(last_solve_kernel, level),
                [(chips, T + height, width)],
                0,
                whole,
                *inverses,
                tip_coupling,
                tip_other,
                *earlier,
            )
        whole_solved = exchanged(solved)
        if level == 0:
            down, up, masks = call(
                first_couple_kernel,
                [(T, width), (T, width), (levels, CORES, columns, width)],
                1,
                pattern,
                whole_solved,
                *couplings,
            )
        else:
            down, up, *tip_message = call(
                functools.partial(couple_kernel, level),
                [(T, width), (T, width)] + [(near, height, width)] * (level == last),
                0,
                masks,
                whole_solved,
                *couplings,
            )
        if level == last - 1:
            down, tip_sent = lax.optimization_barrier((down, tip_coupling))
            tip_other = swapped(tip_sent)
        above = passed(down, "tm", lambda i: (i - stride) % rows)
        below = passed(up, "tm", lambda i: (i + stride) % rows)
        if level < last:
            message, x = call(advance_kernel, [(chips, T, width), (T, width)], 0, x, above, below)
            if level == last - 1:
                message, tip_other = lax.optimization_barrier((message, tip_other))
            whole = exchanged(message)
    tip = lax.all_to_all(
        tip_message[0],
        "tm",
        0,
        0,
        axis_index_groups=[[near * q + i for i in range(near)] for q in range(rows // near)],
        tiled=True,
    ).sum(0)
    keep, send = call(leave_kernel, [(T, T), (T, T)], 0, x, above, below, cost=pl.CostEstimate(flops=2 * 10**10, bytes_accessed=0, transcendentals=0))
    back = swapped(send)
    (reduced,) = call(place_kernel, [(1, T, width)], 0, keep, back)
    count = columns * (rows // near)
    tip_parts = lax.all_to_all(
        jnp.broadcast_to(tip[None], (count, height, width)),
        ("tm", "col"),
        0,
        0,
        axis_index_groups=[
            [(near * q + i) * columns + c for q in range(rows // near) for c in range(columns)] for i in range(near)
        ],
        tiled=True,
    )
    (tip_reduced,) = call(functools.partial(tip_kernel, chips), [(fixed, width)], 0, tip_rhs, tip_parts)
    return reduced, tip_reduced


def solution(mesh):
    return jax.shard_map(
        local,
        mesh=mesh,
        in_specs=(
            P("tm", "col", None),
            P(None, "tm", None, "col"),
            P(None, "tm", None, "col"),
            P(None, "tm", None, "col"),
            P(None, "tm", None, None, "col"),
            P(None, "tm", None, "col"),
            P(),
        ),
        out_specs=(P("tm", "col", None), P()),
        check_vma=False,
    )
```
